256 devices in a mesh: dp: 4 (over x), ctx: 64 (over y, z, core).
Axes of the slice: x: 4, y: 4, z: 8, core: 2. Of those that a mesh axis runs over, the one named last changes fastest.
Arguments:
- win_query: bfloat16 [4, 16384, 1280], P('dp', 'ctx'), may hold values from -180 to 180
- win_key: bfloat16 [4, 16384, 1280], P('dp', 'ctx'), may hold values from -6 to 6
- win_value: bfloat16 [4, 16384, 1280], P('dp', 'ctx'), may hold values from -6 to 6
- win_grad_out: bfloat16 [4, 16384, 1280], P('dp', 'ctx'), may hold values from -6 to 6
- full_query: bfloat16 [4, 16384, 1280], P('dp', 'ctx'), may hold values from -180 to 180
- full_key: bfloat16 [4, 16384, 1280], P('dp', 'ctx'), may hold values from -6 to 6
- full_value: bfloat16 [4, 16384, 1280], P('dp', 'ctx'), may hold values from -6 to 6
- full_grad_out: bfloat16 [4, 16384, 1280], P('dp', 'ctx'), may hold values from -3 to 3
- proj_weight: bfloat16 [1280, 1280], P('ctx'), may hold values from -0.15625 to 0.15625
- positions: int32 [2, 4, 16384], P(None, 'dp', 'ctx'), may hold values from 0 to 31
- tile_perm: int32 [4, 16, 16], P('dp'), may hold values from 0 to 15, each once within a row
- tile_counts: int32 [4, 16, 4], P('dp'), may hold values from 1 to 8, 16 in all within a row
Outputs:
- win_dquery: bfloat16 [4, 32768, 1280], P('dp', 'ctx')
- win_dkey: bfloat16 [4, 32768, 1280], P('dp', 'ctx')
- win_dvalue: bfloat16 [4, 32768, 1280], P('dp', 'ctx')
- full_dquery: bfloat16 [4, 16384, 1280], P('dp', 'ctx')
- full_dkey: bfloat16 [4, 16384, 1280], P('dp', 'ctx')
- full_dvalue: bfloat16 [4, 16384, 1280], P('dp', 'ctx')
- proj_dweight: float32 [1280, 1280], P('ctx')
The draws below stay inside these ranges and needn't reach their ends.
Inputs may be any that keep to these rules, and one draw needn't show every extreme that they name: `tile_perm`: each row names every tile of its slice once. `tile_counts`: the 4 counts of a slice sum to 16, and in every draw some owner takes exactly 8.
All inputs are finite; a program needn't handle non-finite values.
Results may differ from the reference program's by a relative error of at most 0.013.
Values may be sent and summed in bfloat16 or wider, within the bound.
No kernel may reach another device: no remote copies, remote signals or barrier semaphores. Data moves between devices by JAX's collectives and lax.ppermute only.
A program may use at most 128 MiB of HBM per device.

```python
import math
import jax
import jax.numpy as jnp
import numpy as np
from jax import lax

HEADS = 16
HEAD_DIM = 80
SIDE = 32
WIN = 8
D = 1280
SLICE = 1024
TILES = 16
GROUP = 4
CAP = 8
VIDEOS = 4
SEQ = 16384
SLICES = 16
OWNED = 32768


def shared_keys(key, salt):
    return jnp.clip(jax.random.normal(jax.random.fold_in(key, salt), (VIDEOS, SEQ, D), jnp.float32), -6.0, 6.0)


def draw_win_key(key, part):
    shared = shared_keys(key, 101)
    return shared.astype(jnp.bfloat16)


def draw_full_key(key, part):
    shared = shared_keys(key, 102)
    return shared.astype(jnp.bfloat16)


def draw_win_query(key, part):
    key = jax.random.fold_in(key, 2)
    values = jnp.clip(jax.random.normal(key, (VIDEOS, SEQ, D), jnp.float32), -6.0, 6.0)
    return values.astype(jnp.bfloat16)


def draw_full_query(key, part):
    key = jax.random.fold_in(key, 4)
    values = jnp.clip(jax.random.normal(key, (VIDEOS, SEQ, D), jnp.float32), -6.0, 6.0)
    return values.astype(jnp.bfloat16)


def plant(drawn, key, low, largest):
    longest = drawn.shape.index(max(drawn.shape))
    spots = []
    for shift in (0, 1):
        where = [jax.random.randint(jax.random.fold_in(key, axis), (), 0, length) for axis, length in enumerate(drawn.shape)]
        where[longest] = (where[longest] + shift) % drawn.shape[longest]
        spots.append(tuple(where))
    return drawn.at[spots[0]].set(low).at[spots[1]].set(largest)


def block_levels(key, extent, cuts, smallest, high):
    factor_of, own = 1.0, jax.random.fold_in(key, 6)
    for axis_at, parts in cuts:
        heights = jnp.exp(jax.random.uniform(jax.random.fold_in(own, axis_at), (parts,), jnp.float32, smallest / len(cuts), high / len(cuts)))
        factor_of = factor_of * jnp.repeat(heights, extent[axis_at] // parts).reshape([-1 if axis == axis_at else 1 for axis in range(len(extent))])
    return factor_of


def profile(number_of, total, most, skew):
    loads = [(1 << 20) // math.isqrt(rank ** skew) + 1 for rank in range(2, number_of + 1)]
    spare, holding = total - most - (number_of - 1), [1] * (number_of - 1)
    while spare > 0:
        candidates = [i for i in range(number_of - 1) if holding[i] < most]
        pool, budget = sum([loads[i] for i in candidates]), spare
        for i in candidates:
            more = min(most - holding[i], max(1, budget * loads[i] // pool), spare)
            holding[i] = holding[i] + more
            spare = spare - more
    return np.array([most] + holding)


def uneven(stream_key, amount, total, limit, slope):
    if amount == 2:
        one = jax.random.randint(stream_key, (), max(1, total - limit), min(limit, total - 1) + 1)
        return jnp.stack([one, total - one])
    lengths = jnp.asarray(profile(amount, total, limit, slope), jnp.int32)
    pairs = (amount - 1) // 2
    source_of, sink = lengths[1:1 + 2 * pairs:2], lengths[2:2 + 2 * pairs:2]
    room = jnp.minimum(source_of - 1, limit - sink)
    moved = jax.random.randint(jax.random.fold_in(stream_key, 1), (pairs,), 0, 1 << 20) % (room + 1)
    lengths = lengths.at[1:1 + 2 * pairs:2].set(source_of - moved).at[2:2 + 2 * pairs:2].set(sink + moved)
    return lengths[jax.random.permutation(jax.random.fold_in(stream_key, 2), amount)]


def bell_draw(own_key, shape, scale, reach, shards=(), dtype=jnp.bfloat16):
    factor_of = block_levels(own_key, shape, shards, -0.22, 0.18) if shards else 1.0
    values = jax.random.normal(own_key, shape, jnp.float32) * scale * factor_of
    return jnp.minimum(jnp.maximum(values, -reach), reach).astype(dtype)


def setup_inputs(seed: int = 0) -> dict:
    seeds = jax.random.split(jax.random.key(seed), 13)
    return {
        "win_query": draw_win_query(jax.random.fold_in(seeds[12], 71), 0),
        "win_key": draw_win_key(jax.random.fold_in(seeds[12], 71), 0),
        "win_value": bell_draw(seeds[2], (VIDEOS, SEQ, D), 1.0, 6.0, ((0, 4), (1, 64))),
        "win_grad_out": bell_draw(seeds[3], (VIDEOS, SEQ, D), 1.0, 6.0, ((0, 4), (1, 64))),
        "full_query": draw_full_query(jax.random.fold_in(seeds[12], 71), 0),
        "full_key": draw_full_key(jax.random.fold_in(seeds[12], 71), 0),
        "full_value": bell_draw(seeds[6], (VIDEOS, SEQ, D), 1.0, 6.0, ((0, 4), (1, 64))),
        "full_grad_out": bell_draw(seeds[7], (VIDEOS, SEQ, D), 0.5, 3.0, ((0, 4), (1, 64))),
        "proj_weight": bell_draw(seeds[8], (D, D), D ** -0.5, 0.15625, ((0, 64),)),
        "positions": plant(jax.random.randint(seeds[9], (2, VIDEOS, SEQ), 0, SIDE), jax.random.fold_in(seeds[9], 1), 0, SIDE - 1).astype(jnp.int32),
        "tile_perm": jax.vmap(lambda own: jax.random.permutation(own, TILES))(jax.random.split(seeds[10], VIDEOS * SLICES)).reshape((VIDEOS, SLICES, TILES)).astype(jnp.int32),
        "tile_counts": jax.vmap(lambda own: uneven(own, GROUP, TILES, CAP, 2))(jax.random.split(seeds[11], VIDEOS * SLICES)).reshape((VIDEOS, SLICES, GROUP)).astype(jnp.int32),
    }


def rotary_tables(row_index, col_index):
    quarter = HEAD_DIM // 4
    inverse = 1.0 / (10000.0 ** (jnp.arange(quarter).astype(jnp.float32) * 4.0 / HEAD_DIM))
    angle = jnp.concatenate([row_index[..., None] * inverse, col_index[..., None] * inverse], -1)
    angle = jnp.concatenate([angle, angle], -1)
    return jnp.cos(angle), jnp.sin(angle)


def half_turn(tensor):
    middle = tensor.shape[-1] // 2
    return jnp.concatenate([-tensor[..., middle:], tensor[..., :middle]], -1)


def half_turn_back(tensor):
    middle = tensor.shape[-1] // 2
    return jnp.concatenate([tensor[..., middle:], -tensor[..., :middle]], -1)


def rotate(tensor, cos_table, sin_table):
    return tensor * cos_table[..., None, :] + half_turn(tensor) * sin_table[..., None, :]


def unrotate(tensor, cos_table, sin_table):
    return tensor * cos_table[..., None, :] + half_turn_back(tensor * sin_table[..., None, :])


def rounded(tensor):
    return lax.optimization_barrier(tensor.astype(jnp.bfloat16)).astype(jnp.float32)


def attend_backward(query_rows, incoming_keys, incoming_values, incoming_gradient):
    logit_scale = HEAD_DIM ** -0.5
    attention_logits = jnp.einsum("tyj,cyj->ytc", query_rows, incoming_keys) * logit_scale
    attn_probs = jax.nn.softmax(attention_logits, -1)
    probability_reduced = rounded(attn_probs)
    attention_output = jnp.einsum("sjx,xso->jso", probability_reduced, incoming_values)
    probability_gradient = jnp.einsum("tyj,cyj->ytc", incoming_gradient, incoming_values)
    center = jnp.sum(incoming_gradient * attention_output, -1).T
    dscores = attn_probs * (probability_gradient - center[:, :, None])
    score_gradient_reduced = rounded(dscores)
    query_gradient_rows = jnp.einsum("sjx,xso->jso", score_gradient_reduced, incoming_keys) * logit_scale
    key_gradient_rows = jnp.einsum("fqe,qfv->efv", score_gradient_reduced, query_rows) * logit_scale
    value_gradient_rows = jnp.einsum("fqe,qfv->efv", probability_reduced, incoming_gradient)
    return attention_output, query_gradient_rows, key_gradient_rows, value_gradient_rows


def reference(win_query, win_key, win_value, win_grad_out, full_query, full_key, full_value, full_grad_out, proj_weight, positions, tile_perm, tile_counts):
    cos_table, sin_table = rotary_tables(positions[0].astype(jnp.float32), positions[1].astype(jnp.float32))

    def split(tensor):
        return tensor.astype(jnp.float32).reshape(VIDEOS, SEQ, HEADS, HEAD_DIM)

    def turned(tensor):
        return rounded(rotate(split(tensor), cos_table, sin_table))

    win_q = turned(win_query)
    win_k = turned(win_key)
    full_q = turned(full_query)
    full_k = turned(full_key)
    tile_rows = WIN * WIN

    def tiled(tensor):
        return tensor.reshape((SEQ // tile_rows, tile_rows) + tensor.shape[1:])

    def window_video(inputs):
        query_in, key_in, value_in, incoming_gradient, cos_in, sin_in = inputs
        attention_output, query_gradient_rows, key_gradient_rows, value_gradient_rows = jax.vmap(attend_backward)(tiled(query_in), tiled(key_in), tiled(value_in), tiled(incoming_gradient))
        query_gradient_rows = unrotate(query_gradient_rows, tiled(cos_in), tiled(sin_in))
        key_gradient_rows = unrotate(key_gradient_rows, tiled(cos_in), tiled(sin_in))
        return tuple(piece_out.astype(jnp.bfloat16).reshape(SEQ, D) for piece_out in (query_gradient_rows, key_gradient_rows, value_gradient_rows))

    window_q, window_k, window_v = lax.map(window_video, (win_q, win_k, split(win_value), split(win_grad_out), cos_table, sin_table))

    slice_count = SEQ // SLICE
    before = (jnp.cumsum(tile_counts, -1) - tile_counts).astype(jnp.int32)
    slot_ids = jnp.arange(CAP).astype(jnp.int32)
    picks = jnp.minimum(before[..., None] + slot_ids, TILES - 1).astype(jnp.int32)
    chosen = jax.vmap(jax.vmap(lambda order_row, where_at: order_row[where_at]))(tile_perm, picks)
    slot_live = slot_ids < tile_counts[..., None]

    def owned(grads_in):
        tiles_view = grads_in.reshape(VIDEOS, slice_count, TILES, tile_rows, D)
        picked = jax.vmap(jax.vmap(lambda table, where_at: table[where_at]))(tiles_view, chosen)
        picked = jnp.where(slot_live[..., None, None], picked, jnp.zeros_like(picked))
        return picked.reshape(VIDEOS, OWNED, D)

    dattn = jnp.dot(full_grad_out.reshape(VIDEOS * SEQ, D), proj_weight.T, preferred_element_type=jnp.float32)
    dattn = rounded(dattn).reshape(VIDEOS, SEQ, HEADS, HEAD_DIM)

    def by_slice(tensor):
        return tensor.reshape((VIDEOS * slice_count, SLICE) + tensor.shape[2:])

    def full_slice(inputs):
        query_in, key_in, value_in, incoming_gradient, cos_in, sin_in = inputs
        attention_output, query_gradient_rows, key_gradient_rows, value_gradient_rows = attend_backward(query_in, key_in, value_in, incoming_gradient)
        query_gradient_rows = unrotate(query_gradient_rows, cos_in, sin_in)
        key_gradient_rows = unrotate(key_gradient_rows, cos_in, sin_in)
        return tuple(piece_out.astype(jnp.bfloat16).reshape(SLICE, D) for piece_out in (attention_output, query_gradient_rows, key_gradient_rows, value_gradient_rows))

    out_low, full_dq, full_dk, full_dv = lax.map(full_slice, (by_slice(full_q), by_slice(full_k), by_slice(split(full_value)), by_slice(dattn), by_slice(cos_table), by_slice(sin_table)))
    proj_dweight = jnp.dot(out_low.reshape(VIDEOS * SEQ, D).T, full_grad_out.reshape(VIDEOS * SEQ, D), preferred_element_type=jnp.float32)
    return (owned(window_q), owned(window_k), owned(window_v), full_dq.reshape(VIDEOS, SEQ, D), full_dk.reshape(VIDEOS, SEQ, D), full_dv.reshape(VIDEOS, SEQ, D), proj_dweight)
```

```python
import functools

import jax
import jax.numpy as jnp
from jax import lax
from jax.experimental import pallas as pl
from jax.experimental.pallas import tpu as pltpu
from jax.sharding import PartitionSpec as P

HEADS = 16
HEAD_DIM = 80
HALF = HEAD_DIM // 2
TILE = 64
TILES = 16
GROUP = 4
CAP = 8
D = HEADS * HEAD_DIM
QUARTER = D // GROUP
SCALE = HEAD_DIM**-0.5
SCALE2 = SCALE * 1.4426950408889634
BF = jnp.bfloat16
F32 = jnp.float32
VM = pl.BlockSpec(memory_space=pltpu.VMEM)
SM = pl.BlockSpec(memory_space=pltpu.SMEM)
HINT = pl.CostEstimate(flops=100_000, bytes_accessed=100_000, transcendentals=0)


def params(mib=56):
    return pltpu.CompilerParams(vmem_limit_bytes=mib << 20)


def dot(left, right, left_dim, right_dim):
    return lax.dot_general(
        left, right, (((left_dim,), (right_dim,)), ((), ())), preferred_element_type=F32
    )


def turn(rows, cos, sin):
    low, high = rows[:HALF], rows[HALF:]
    return jnp.concatenate([low * cos - high * sin, high * cos + low * sin], 0)


def turn_back(rows, cos, sin):
    low, high = rows[:HALF], rows[HALF:]
    return jnp.concatenate([low * cos + high * sin, high * cos - low * sin], 0)


def load_turned(source, target, scratch, cos, sin):
    width = source.shape[1]
    for block in range(0, width, 128):
        scratch[block : block + 128, :] = source[:, block : block + 128].astype(F32).T
    for head in range(0, width, HEAD_DIM):
        rows = scratch[head : head + HEAD_DIM, :]
        if cos is not None:
            rows = turn(rows, cos, sin)
        target[head : head + HEAD_DIM, :] = rows.astype(BF)


def store_natural(scratch, target):
    for block in range(0, scratch.shape[0], 128):
        target[:, block : block + 128] = scratch[block : block + 128, :].T.astype(BF)


def split_kernel(place, query, key, value, cos_ref, sin_ref, out0, out1, out2, out3, scratch, qt, kt, vt):
    cos, sin = cos_ref[...], sin_ref[...]
    load_turned(query, qt, scratch, cos, sin)
    load_turned(key, kt, scratch, cos, sin)
    load_turned(value, vt, scratch, None, None)
    member = place[0]
    for step, out in enumerate((out0, out1, out2, out3)):
        for part, source in enumerate((qt, kt, vt)):
            for block in range(GROUP):
                start = pl.multiple_of((member ^ step) * HEAD_DIM + block * QUARTER, HEAD_DIM)
                target = part * QUARTER + block * HEAD_DIM
                out[target : target + HEAD_DIM, :] = source[pl.ds(start, HEAD_DIM), :]


def split_heads(place, query, key, value, cos, sin):
    rows = query.shape[0]
    return pl.pallas_call(
        split_kernel,
        out_shape=[jax.ShapeDtypeStruct((3 * QUARTER, rows), BF)] * GROUP,
        in_specs=[SM] + [VM] * 5,
        out_specs=[VM] * GROUP,
        scratch_shapes=[pltpu.VMEM((D, rows), F32)] + [pltpu.VMEM((D, rows), BF)] * 3,
        compiler_params=params(),
        cost_estimate=HINT,
        name="split_heads",
    )(place, query, key, value, cos, sin)


def window_kernel(place, query, key, value, grad, cos_ref, sin_ref, *refs):
    del place
    outs, (scratch, qt, kt, vt, gt, dqt, dkt, dvt) = refs[:-8], refs[-8:]
    cos, sin = cos_ref[...], sin_ref[...]
    load_turned(query, qt, scratch, cos, sin)
    load_turned(key, kt, scratch, cos, sin)
    load_turned(value, vt, scratch, None, None)
    load_turned(grad, gt, scratch, None, None)
    rows, width = query.shape
    same = (
        lax.broadcasted_iota(jnp.int32, (rows, rows), 0) // TILE
        == lax.broadcasted_iota(jnp.int32, (rows, rows), 1) // TILE
    )

    def head_step(head, carry):
        here = pl.ds(pl.multiple_of(head * HEAD_DIM, HEAD_DIM), HEAD_DIM)
        q, k, v, g = qt[here, :], kt[here, :], vt[here, :], gt[here, :]
        logits = jnp.where(same, dot(k, q, 0, 0), -1e30)
        raised = jnp.exp2((logits - jnp.max(logits, 0, keepdims=True)) * SCALE2)
        inverse = 1.0 / jnp.sum(raised, 0, keepdims=True)
        low = raised.astype(BF)
        g = (g.astype(F32) * inverse).astype(BF)
        center = jnp.sum(g.astype(F32) * (dot(v, low, 1, 0) * inverse), 0, keepdims=True)
        dscores = (raised * (dot(v, g, 0, 0) - center)).astype(BF)
        dqt[here, :] = turn_back(dot(k, dscores, 1, 0) * SCALE, cos, sin)
        dkt[here, :] = turn_back(dot(q, dscores, 1, 1) * SCALE, cos, sin)
        dvt[here, :] = dot(g, low, 1, 1)
        return carry

    lax.fori_loop(0, width // HEAD_DIM, head_step, 0, unroll=2)
    places = [out.at[at : at + rows] for out in outs for at in range(0, out.shape[0], rows)]
    for source, target in zip((dqt, dkt, dvt), places):
        store_natural(source, target)


def window_grads(place, query, key, value, grad, cos, sin, half, packs):
    rows, width = query.shape[0], D // 2
    block = pl.BlockSpec((rows, width), lambda step: (0, half))
    return pl.pallas_call(
        window_kernel,
        grid=(1,),
        out_shape=[jax.ShapeDtypeStruct((pack * rows, width), BF) for pack in packs],
        in_specs=[SM] + [block] * 4 + [VM] * 2,
        out_specs=[VM] * len(packs),
        scratch_shapes=[pltpu.VMEM((width, rows), F32)] + [pltpu.VMEM((width, rows), BF)] * 4 + [pltpu.VMEM((width, rows), F32)] * 3,
        compiler_params=params(),
        cost_estimate=HINT,
        name="window_grads",
    )(place, query, key, value, grad, cos, sin)


def heads_of(pieces, first, part, width):
    rows = pl.ds(pl.multiple_of(first + part * width, 16), HEAD_DIM)
    return jnp.concatenate([piece[rows, :] for piece in pieces], 1)


def probs_kernel(place, piece0, piece1, piece2, piece3, raised_low, out, inverses):
    del place
    pieces = (piece0, piece1, piece2, piece3)
    rows = piece0.shape[1]
    first = pl.multiple_of(pl.program_id(0) * HEAD_DIM, HEAD_DIM)
    here = pl.ds(first, HEAD_DIM)
    k_rows, v = heads_of(pieces, first, 1, QUARTER).T, heads_of(pieces, first, 2, QUARTER)
    for step in range(GROUP):
        block = slice(step * rows, (step + 1) * rows)
        logits = dot(k_rows, pieces[step][here, :], 1, 0)
        raised = jnp.exp2((logits - jnp.max(logits, 0, keepdims=True)) * SCALE2)
        inverse = 1.0 / jnp.sum(raised, 0, keepdims=True)
        low = raised.astype(BF)
        raised_low[0, :, block] = low
        inverses[pl.program_id(0), :, block] = inverse
        out[here, block] = dot(v, low, 1, 0) * inverse


def full_probs(place, pieces):
    length = GROUP * pieces[0].shape[1]
    heads = HEADS // GROUP
    return pl.pallas_call(
        probs_kernel,
        grid=(heads,),
        out_shape=[
            jax.ShapeDtypeStruct((heads, length, length), BF),
            jax.ShapeDtypeStruct((QUARTER, length), F32),
            jax.ShapeDtypeStruct((heads, 1, length), F32),
        ],
        in_specs=[SM] + [VM] * 4,
        out_specs=[pl.BlockSpec((1, length, length), lambda head: (head, 0, 0)), VM, VM],
        compiler_params=params(),
        cost_estimate=HINT,
        name="full_probs",
    )(place, *pieces)


def share_kernel(*refs):
    place, out, grads, weights, shares, dattn = refs[0], refs[1], refs[2:6], refs[6:10], refs[10:14], refs[14]
    product, weight = refs[15:]
    rows = grads[0].shape[0]
    starts = [pl.multiple_of((place[1] ^ step) * HEAD_DIM, HEAD_DIM) for step in range(GROUP)]
    for step in range(GROUP):
        weight[pl.ds(starts[step], HEAD_DIM), :] = weights[step][...]
    for step in range(GROUP):
        block = slice(step * rows, (step + 1) * rows)
        dattn[:, block] = dot(weight[...], grads[step][...], 1, 1).astype(BF)
        share = dot(out[:, block].astype(BF), grads[step][...], 1, 0)
        product[...] = share if step == 0 else product[...] + share
    for step in range(GROUP):
        shares[step][...] = product[pl.ds(starts[step], HEAD_DIM), :].astype(BF)


def weight_shares(place, out, grads, weights):
    return pl.pallas_call(
        share_kernel,
        out_shape=[jax.ShapeDtypeStruct((HEAD_DIM, D), BF)] * GROUP + [jax.ShapeDtypeStruct(out.shape, BF)],
        in_specs=[SM] + [VM] * 9,
        out_specs=[VM] * 5,
        scratch_shapes=[pltpu.VMEM((QUARTER, D), F32), pltpu.VMEM((QUARTER, D), BF)],
        compiler_params=params(),
        cost_estimate=HINT,
        name="weight_shares",
    )(place, out, *grads, *weights)


def grads_kernel(*refs):
    pieces, dattn, out, inverses, raised_low, backs = refs[1:5], refs[5], refs[6], refs[7], refs[8], refs[9:]
    rows = pieces[0].shape[1]
    first = pl.multiple_of(pl.program_id(0) * HEAD_DIM, HEAD_DIM)
    here = pl.ds(first, HEAD_DIM)
    k, v_rows = heads_of(pieces, first, 1, QUARTER), heads_of(pieces, first, 2, QUARTER).T
    dk = jnp.zeros((HEAD_DIM, GROUP * rows), F32)
    dv = jnp.zeros((HEAD_DIM, GROUP * rows), F32)
    for step in range(GROUP):
        block = slice(step * rows, (step + 1) * rows)
        q, low = pieces[step][here, :], raised_low[0, :, block]
        g = (dattn[here, block].astype(F32) * inverses[pl.program_id(0), :, block]).astype(BF)
        center = jnp.sum(g.astype(F32) * out[here, block], 0, keepdims=True)
        dscores = (low.astype(F32) * (dot(v_rows, g, 1, 0) - center)).astype(BF)
        backs[step][here, :] = (dot(k, dscores, 1, 0) * SCALE).astype(BF)
        dk += dot(q, dscores, 1, 1)
        dv += dot(g, low, 1, 1)
    for step in range(GROUP):
        block = slice(step * rows, (step + 1) * rows)
        backs[step][pl.ds(pl.multiple_of(first + QUARTER, 16), HEAD_DIM), :] = (dk[:, block] * SCALE).astype(BF)
        backs[step][pl.ds(pl.multiple_of(first + 2 * QUARTER, 16), HEAD_DIM), :] = dv[:, block].astype(BF)


def full_grads(place, pieces, dattn, out, inverses, raised_low):
    rows = pieces[0].shape[1]
    length = GROUP * rows
    return pl.pallas_call(
        grads_kernel,
        grid=(HEADS // GROUP,),
        out_shape=[jax.ShapeDtypeStruct((3 * QUARTER, rows), BF)] * GROUP,
        in_specs=[SM] + [VM] * 7 + [pl.BlockSpec((1, length, length), lambda head: (head, 0, 0))],
        out_specs=[VM] * GROUP,
        compiler_params=params(),
        cost_estimate=HINT,
        name="full_grads",
    )(place, *pieces, dattn, out, inverses, raised_low)


def join_kernel(place, part0, part1, part2, part3, cos_ref, sin_ref, dquery, dkey, dvalue, scratch):
    cos, sin = cos_ref[...], sin_ref[...]
    member = place[0]
    for which, target in enumerate((dquery, dkey, dvalue)):
        for step, part in enumerate((part0, part1, part2, part3)):
            for block in range(GROUP):
                source = which * QUARTER + block * HEAD_DIM
                rows = part[source : source + HEAD_DIM, :].astype(F32)
                if which < 2:
                    rows = turn_back(rows, cos, sin)
                start = pl.multiple_of((member ^ step) * HEAD_DIM + block * QUARTER, HEAD_DIM)
                scratch[pl.ds(start, HEAD_DIM), :] = rows
        store_natural(scratch, target)


def join_heads(place, parts, cos, sin):
    rows = parts[0].shape[1]
    return pl.pallas_call(
        join_kernel,
        out_shape=[jax.ShapeDtypeStruct((rows, D), BF)] * 3,
        in_specs=[SM] + [VM] * 6,
        out_specs=[VM] * 3,
        scratch_shapes=[pltpu.VMEM((D, rows), F32)],
        compiler_params=params(),
        cost_estimate=HINT,
        name="join_heads",
    )(place, *parts, cos, sin)


def deal_kernel(starts, place, perm, counts, *refs):
    sources, out = (refs[:GROUP], refs[GROUP : 2 * GROUP]), refs[2 * GROUP]
    member, slice_id = place[0], place[2]
    width = sources[0][0].shape[1]
    before = jnp.int32(0)
    for owner in range(GROUP - 1):
        before += jnp.where(owner < member, counts[slice_id, owner], 0)
    taken = counts[slice_id, member]
    for slot in range(CAP):
        tile = perm[slice_id, jnp.minimum(before + slot, TILES - 1)]
        live = slot < taken
        where = (tile // GROUP) ^ member
        row = (tile % GROUP) * TILE
        target = slice(slot * TILE, (slot + 1) * TILE)
        for step in range(GROUP):

            @pl.when(live & (where == step))
            def _():
                for half, pieces in enumerate(sources):
                    here = pl.ds(pl.multiple_of(row + starts[half], TILE), TILE)
                    out[target, half * width : (half + 1) * width] = pieces[step][here, :]

        @pl.when(jnp.logical_not(live))
        def _():
            out[target, :] = jnp.zeros((TILE, out.shape[1]), BF)


def deal_tiles(place, perm, counts, first, second, starts):
    return pl.pallas_call(
        functools.partial(deal_kernel, starts),
        out_shape=jax.ShapeDtypeStruct((CAP * TILE, D), BF),
        in_specs=[SM] * 3 + [VM] * 8,
        out_specs=VM,
        compiler_params=params(),
        cost_estimate=HINT,
        name="deal_tiles",
    )(place, perm, counts, *first, *second)


def swap(array, axis, distance):
    count = lax.axis_size(axis)
    return lax.ppermute(array, axis, [(i, i ^ distance) for i in range(count)])


def rotary_tables(row_index, col_index):
    quarter = HEAD_DIM // 4
    inverse = 1.0 / 10000.0 ** (jnp.arange(quarter).astype(F32) * 4.0 / HEAD_DIM)
    angle = jnp.concatenate([inverse[:, None] * row_index[None], inverse[:, None] * col_index[None]], 0)
    return jnp.cos(angle), jnp.sin(angle)


def relabel(count, pair):
    where = lambda x, y, s, m: ((x * count + y) * count + s) * count + m
    span = range(count)
    route = [pair(x, y, s, m) for x in span for y in span for s in span for m in span]
    return [(where(*source), where(*target)) for source, target in route]


def gather_route(count):
    return relabel(count, lambda x, y, s, m: ((s, y, m, x), (x, y, s, m)))


def share_route(count, step):
    return relabel(count, lambda x, y, s, m: ((x, y, s, m), (s ^ step, y, m, x)))


def shards(
    win_query,
    win_key,
    win_value,
    win_grad_out,
    full_query,
    full_key,
    full_value,
    full_grad_out,
    proj_weight,
    positions,
    tile_perm,
    tile_counts,
):
    index = lax.axis_index("ctx")
    member, slice_id = index % GROUP, index // GROUP
    plane = slice_id // GROUP
    across = lax.axis_index("dp")
    place = jnp.stack([member, plane, slice_id]).astype(jnp.int32)
    tie = lax.optimization_barrier

    def total(arrays):
        return sum((array.astype(F32) for array in arrays[1:]), arrays[0].astype(F32))

    corner = lax.ppermute(proj_weight, ("dp", "ctx"), gather_route(GROUP))
    cos, sin = rotary_tables(positions[0, 0].astype(F32), positions[1, 0].astype(F32))
    pieces = split_heads(place, full_query[0], full_key[0], full_value[0], cos, sin)

    place, *pieces = tie((place, *pieces))
    piece1, piece2 = swap(pieces[1], "ctx", 1), swap(pieces[2], "ctx", 2)
    window_in = (win_query[0], win_key[0], win_value[0], win_grad_out[0], cos, sin)
    first = window_grads(place, *window_in, 0, (3,))

    place, first, corner, piece1, piece2, sent3 = tie((place, first, corner, piece1, piece2, pieces[3]))
    piece3 = swap(sent3, "ctx", 3)
    corners = [corner] + [swap(corner, "dp", step) for step in range(1, GROUP)]
    second = window_grads(place, *window_in, 1, (2, 1))

    place, first, second, piece3, corners, grad0 = tie((place, first, second, piece3, corners, full_grad_out[0]))
    pieces = (pieces[0], piece1, piece2, piece3)
    grad1, grad2 = swap(grad0, "ctx", 1), swap(grad0, "ctx", 2)
    low_bit, high_bit = across % 2 == 1, across // 2 == 1
    pairs = [jnp.where(low_bit, corners[i ^ 1], corners[i]) for i in range(GROUP)]
    weight0 = jnp.concatenate([jnp.where(high_bit, pairs[i ^ 2], pairs[i]) for i in range(GROUP)], 0)
    weights = [weight0] + [swap(weight0, "ctx", step * 16) for step in range(1, GROUP)]
    window = [*first, *second]
    raised_low, out, inverses = full_probs(place, pieces)

    place, raised_low, out, grad1, grad2, weights, window = tie(
        (place, raised_low, out, grad1, grad2, weights, window)
    )
    crossed = [swap(window[0], "ctx", 2)]
    grads = (grad0, grad1, grad2, swap(grad2, "ctx", 1))
    *shares, dattn = weight_shares(place, out, grads, weights)

    place, dattn, *shares = tie((place, dattn, *shares))
    crossed.append(swap(window[1], "ctx", 2))
    swapped = [swap(shares[step], "ctx", step * 16) for step in range(1, GROUP)]
    backs = full_grads(place, pieces, dattn, out, inverses, raised_low)

    place, backs, swapped, crossed, window = tie((place, backs, swapped, crossed, window))
    parts = [backs[0]] + [swap(backs[step], "ctx", step) for step in range(1, GROUP)]
    crossed.append(swap(window[2], "ctx", 2))
    sibling = [swap(array, "ctx", 1) for array in window]
    opposite = [swap(array, "ctx", 1) for array in crossed]
    rows = total([shares[0], *swapped]).reshape(GROUP, HEAD_DIM // GROUP, D).astype(BF)
    rows = [lax.dynamic_index_in_dim(rows, across ^ step, 0, keepdims=False) for step in range(GROUP)]
    summed = [rows[0]] + [swap(rows[step], "dp", step) for step in range(1, GROUP)]
    share = total(summed).astype(BF)
    sets = list(zip(window, sibling, crossed, opposite))
    tile_rows = first[0].shape[0] // 3

    def deal(which):
        other, start = (1, which * tile_rows) if which < 2 else (2, 0)
        starts = (which * tile_rows, start)
        return deal_tiles(place, tile_perm[0], tile_counts[0], sets[0], sets[other], starts)[None]

    dealt = [deal(0), deal(1)]
    place, share, parts, opposite, dealt = tie((place, share, parts, opposite, dealt))
    sets = list(zip(window, sibling, crossed, opposite))
    shared = [lax.ppermute(share, ("dp", "ctx"), share_route(GROUP, step)) for step in range(GROUP)]
    dealt.append(deal(2))
    full = join_heads(place, parts, cos, sin)
    return (*dealt, *[array[None] for array in full], total(shared))


def solution(mesh):
    rows = P("dp", "ctx", None)
    in_specs = (rows,) * 8 + (P("ctx", None), P(None, "dp", "ctx"), P("dp", None, None), P("dp", None, None))
    out_specs = (rows,) * 6 + (P("ctx", None),)
    return jax.shard_map(shards, mesh=mesh, in_specs=in_specs, out_specs=out_specs, check_vma=False)
```

```python
import functools

import jax
import jax.numpy as jnp
from jax import lax
from jax.experimental import pallas as pl
from jax.experimental.pallas import tpu as pltpu
from jax.sharding import PartitionSpec as P

HEADS = 16
HEAD_DIM = 80
HALF = HEAD_DIM // 2
TILE = 64
TILES = 16
GROUP = 4
CAP = 8
D = HEADS * HEAD_DIM
QUARTER = D // GROUP
SCALE = HEAD_DIM**-0.5
SCALE2 = SCALE * 1.4426950408889634
BF = jnp.bfloat16
F32 = jnp.float32
VM = pl.BlockSpec(memory_space=pltpu.VMEM)
SM = pl.BlockSpec(memory_space=pltpu.SMEM)
HINT = pl.CostEstimate(flops=100_000, bytes_accessed=100_000, transcendentals=0)


def params(mib=56):
    return pltpu.CompilerParams(vmem_limit_bytes=mib << 20)


def dot(left, right, left_dim, right_dim):
    return lax.dot_general(
        left, right, (((left_dim,), (right_dim,)), ((), ())), preferred_element_type=F32
    )


def turn(rows, cos, sin):
    low, high = rows[:HALF], rows[HALF:]
    return jnp.concatenate([low * cos - high * sin, high * cos + low * sin], 0)


def turn_back(rows, cos, sin):
    low, high = rows[:HALF], rows[HALF:]
    return jnp.concatenate([low * cos + high * sin, high * cos - low * sin], 0)


def load_turned(source, target, scratch, cos, sin):
    width = source.shape[1]
    for block in range(0, width, 128):
        scratch[block : block + 128, :] = source[:, block : block + 128].astype(F32).T
    for head in range(0, width, HEAD_DIM):
        rows = scratch[head : head + HEAD_DIM, :]
        if cos is not None:
            rows = turn(rows, cos, sin)
        target[head : head + HEAD_DIM, :] = rows.astype(BF)


def store_natural(scratch, target):
    for block in range(0, scratch.shape[0], 128):
        target[:, block : block + 128] = scratch[block : block + 128, :].T.astype(BF)


def split_kernel(place, query, key, value, cos_ref, sin_ref, out0, out1, out2, out3, scratch, qt, kt, vt):
    cos, sin = cos_ref[...], sin_ref[...]
    load_turned(query, qt, scratch, cos, sin)
    load_turned(key, kt, scratch, cos, sin)
    load_turned(value, vt, scratch, None, None)
    member = place[0]
    for step, out in enumerate((out0, out1, out2, out3)):
        for part, source in enumerate((qt, kt, vt)):
            for block in range(GROUP):
                start = pl.multiple_of((member ^ step) * HEAD_DIM + block * QUARTER, HEAD_DIM)
                target = part * QUARTER + block * HEAD_DIM
                out[target : target + HEAD_DIM, :] = source[pl.ds(start, HEAD_DIM), :]


def split_heads(place, query, key, value, cos, sin):
    rows = query.shape[0]
    return pl.pallas_call(
        split_kernel,
        out_shape=[jax.ShapeDtypeStruct((3 * QUARTER, rows), BF)] * GROUP,
        in_specs=[SM] + [VM] * 5,
        out_specs=[VM] * GROUP,
        scratch_shapes=[pltpu.VMEM((D, rows), F32)] + [pltpu.VMEM((D, rows), BF)] * 3,
        compiler_params=params(),
        cost_estimate=HINT,
        name="split_heads",
    )(place, query, key, value, cos, sin)


def window_kernel(place, query, key, value, grad, cos_ref, sin_ref, *refs):
    del place
    outs, (scratch, qt, kt, vt, gt, dqt, dkt, dvt) = refs[:-8], refs[-8:]
    cos, sin = cos_ref[...], sin_ref[...]
    load_turned(query, qt, scratch, cos, sin)
    load_turned(key, kt, scratch, cos, sin)
    load_turned(value, vt, scratch, None, None)
    load_turned(grad, gt, scratch, None, None)
    rows, width = query.shape
    same = (
        lax.broadcasted_iota(jnp.int32, (rows, rows), 0) // TILE
        == lax.broadcasted_iota(jnp.int32, (rows, rows), 1) // TILE
    )

    def head_step(head, carry):
        here = pl.ds(pl.multiple_of(head * HEAD_DIM, HEAD_DIM), HEAD_DIM)
        q, k, v, g = qt[here, :], kt[here, :], vt[here, :], gt[here, :]
        logits = jnp.where(same, dot(k, q, 0, 0), -1e30)
        raised = jnp.exp2((logits - jnp.max(logits, 0, keepdims=True)) * SCALE2)
        inverse = 1.0 / jnp.sum(raised, 0, keepdims=True)
        low = raised.astype(BF)
        g = (g.astype(F32) * inverse).astype(BF)
        center = jnp.sum(g.astype(F32) * (dot(v, low, 1, 0) * inverse), 0, keepdims=True)
        dscores = (raised * (dot(v, g, 0, 0) - center)).astype(BF)
        dqt[here, :] = turn_back(dot(k, dscores, 1, 0) * SCALE, cos, sin)
        dkt[here, :] = turn_back(dot(q, dscores, 1, 1) * SCALE, cos, sin)
        dvt[here, :] = dot(g, low, 1, 1)
        return carry

    lax.fori_loop(0, width // HEAD_DIM, head_step, 0, unroll=2)
    places = [out.at[at : at + rows] for out in outs for at in range(0, out.shape[0], rows)]
    for source, target in zip((dqt, dkt, dvt), places):
        store_natural(source, target)


def window_grads(place, query, key, value, grad, cos, sin, half, packs):
    rows, width = query.shape[0], D // 2
    block = pl.BlockSpec((rows, width), lambda step: (0, half))
    return pl.pallas_call(
        window_kernel,
        grid=(1,),
        out_shape=[jax.ShapeDtypeStruct((pack * rows, width), BF) for pack in packs],
        in_specs=[SM] + [block] * 4 + [VM] * 2,
        out_specs=[VM] * len(packs),
        scratch_shapes=[pltpu.VMEM((width, rows), F32)] + [pltpu.VMEM((width, rows), BF)] * 4 + [pltpu.VMEM((width, rows), F32)] * 3,
        compiler_params=params(),
        cost_estimate=HINT,
        name="window_grads",
    )(place, query, key, value, grad, cos, sin)


def heads_of(pieces, first, part, width):
    rows = pl.ds(pl.multiple_of(first + part * width, 16), HEAD_DIM)
    return jnp.concatenate([piece[rows, :] for piece in pieces], 1)


def probs_kernel(place, piece0, piece1, piece2, piece3, raised_low, out, inverses):
    del place
    pieces = (piece0, piece1, piece2, piece3)
    rows = piece0.shape[1]
    first = pl.multiple_of(pl.program_id(0) * HEAD_DIM, HEAD_DIM)
    here = pl.ds(first, HEAD_DIM)
    k_rows, v = heads_of(pieces, first, 1, QUARTER).T, heads_of(pieces, first, 2, QUARTER)
    for step in range(GROUP):
        block = slice(step * rows, (step + 1) * rows)
        logits = dot(k_rows, pieces[step][here, :], 1, 0)
        raised = jnp.exp2((logits - jnp.max(logits, 0, keepdims=True)) * SCALE2)
        inverse = 1.0 / jnp.sum(raised, 0, keepdims=True)
        low = raised.astype(BF)
        raised_low[0, :, block] = low
        inverses[pl.program_id(0), :, block] = inverse
        out[here, block] = dot(v, low, 1, 0) * inverse


def full_probs(place, pieces):
    length = GROUP * pieces[0].shape[1]
    heads = HEADS // GROUP
    return pl.pallas_call(
        probs_kernel,
        grid=(heads,),
        out_shape=[
            jax.ShapeDtypeStruct((heads, length, length), BF),
            jax.ShapeDtypeStruct((QUARTER, length), F32),
            jax.ShapeDtypeStruct((heads, 1, length), F32),
        ],
        in_specs=[SM] + [VM] * 4,
        out_specs=[pl.BlockSpec((1, length, length), lambda head: (head, 0, 0)), VM, VM],
        compiler_params=params(),
        cost_estimate=HINT,
        name="full_probs",
    )(place, *pieces)


def share_kernel(*refs):
    place, out, grads, weights, shares, dattn = refs[0], refs[1], refs[2:6], refs[6:10], refs[10:14], refs[14]
    product, weight = refs[15:]
    rows = grads[0].shape[0]
    starts = [pl.multiple_of((place[1] ^ step) * HEAD_DIM, HEAD_DIM) for step in range(GROUP)]
    for step in range(GROUP):
        weight[pl.ds(starts[step], HEAD_DIM), :] = weights[step][...]
    for step in range(GROUP):
        block = slice(step * rows, (step + 1) * rows)
        dattn[:, block] = dot(weight[...], grads[step][...], 1, 1).astype(BF)
        share = dot(out[:, block].astype(BF), grads[step][...], 1, 0)
        product[...] = share if step == 0 else product[...] + share
    for step in range(GROUP):
        shares[step][...] = product[pl.ds(starts[step], HEAD_DIM), :].astype(BF)


def weight_shares(place, out, grads, weights):
    return pl.pallas_call(
        share_kernel,
        out_shape=[jax.ShapeDtypeStruct((HEAD_DIM, D), BF)] * GROUP + [jax.ShapeDtypeStruct(out.shape, BF)],
        in_specs=[SM] + [VM] * 9,
        out_specs=[VM] * 5,
        scratch_shapes=[pltpu.VMEM((QUARTER, D), F32), pltpu.VMEM((QUARTER, D), BF)],
        compiler_params=params(),
        cost_estimate=HINT,
        name="weight_shares",
    )(place, out, *grads, *weights)


def grads_kernel(*refs):
    pieces, dattn, out, inverses, raised_low, backs = refs[1:5], refs[5], refs[6], refs[7], refs[8], refs[9:]
    rows = pieces[0].shape[1]
    first = pl.multiple_of(pl.program_id(0) * HEAD_DIM, HEAD_DIM)
    here = pl.ds(first, HEAD_DIM)
    k, v_rows = heads_of(pieces, first, 1, QUARTER), heads_of(pieces, first, 2, QUARTER).T
    dk = jnp.zeros((HEAD_DIM, GROUP * rows), F32)
    dv = jnp.zeros((HEAD_DIM, GROUP * rows), F32)
    for step in range(GROUP):
        block = slice(step * rows, (step + 1) * rows)
        q, low = pieces[step][here, :], raised_low[0, :, block]
        g = (dattn[here, block].astype(F32) * inverses[pl.program_id(0), :, block]).astype(BF)
        center = jnp.sum(g.astype(F32) * out[here, block], 0, keepdims=True)
        dscores = (low.astype(F32) * (dot(v_rows, g, 1, 0) - center)).astype(BF)
        backs[step][here, :] = (dot(k, dscores, 1, 0) * SCALE).astype(BF)
        dk += dot(q, dscores, 1, 1)
        dv += dot(g, low, 1, 1)
    for step in range(GROUP):
        block = slice(step * rows, (step + 1) * rows)
        backs[step][pl.ds(pl.multiple_of(first + QUARTER, 16), HEAD_DIM), :] = (dk[:, block] * SCALE).astype(BF)
        backs[step][pl.ds(pl.multiple_of(first + 2 * QUARTER, 16), HEAD_DIM), :] = dv[:, block].astype(BF)


def full_grads(place, pieces, dattn, out, inverses, raised_low):
    rows = pieces[0].shape[1]
    length = GROUP * rows
    return pl.pallas_call(
        grads_kernel,
        grid=(HEADS // GROUP,),
        out_shape=[jax.ShapeDtypeStruct((3 * QUARTER, rows), BF)] * GROUP,
        in_specs=[SM] + [VM] * 7 + [pl.BlockSpec((1, length, length), lambda head: (head, 0, 0))],
        out_specs=[VM] * GROUP,
        compiler_params=params(),
        cost_estimate=HINT,
        name="full_grads",
    )(place, *pieces, dattn, out, inverses, raised_low)


def join_kernel(place, part0, part1, part2, part3, cos_ref, sin_ref, dquery, dkey, dvalue, scratch):
    cos, sin = cos_ref[...], sin_ref[...]
    member = place[0]
    for which, target in enumerate((dquery, dkey, dvalue)):
        for step, part in enumerate((part0, part1, part2, part3)):
            for block in range(GROUP):
                source = which * QUARTER + block * HEAD_DIM
                rows = part[source : source + HEAD_DIM, :].astype(F32)
                if which < 2:
                    rows = turn_back(rows, cos, sin)
                start = pl.multiple_of((member ^ step) * HEAD_DIM + block * QUARTER, HEAD_DIM)
                scratch[pl.ds(start, HEAD_DIM), :] = rows
        store_natural(scratch, target)


def join_heads(place, parts, cos, sin):
    rows = parts[0].shape[1]
    return pl.pallas_call(
        join_kernel,
        out_shape=[jax.ShapeDtypeStruct((rows, D), BF)] * 3,
        in_specs=[SM] + [VM] * 6,
        out_specs=[VM] * 3,
        scratch_shapes=[pltpu.VMEM((D, rows), F32)],
        compiler_params=params(),
        cost_estimate=HINT,
        name="join_heads",
    )(place, *parts, cos, sin)


def deal_kernel(place, perm, counts, *refs):
    sources, out = (refs[:GROUP], refs[GROUP : 2 * GROUP]), refs[2 * GROUP]
    member, slice_id = place[0], place[2]
    width = sources[0][0].shape[1]
    before = jnp.int32(0)
    for owner in range(GROUP - 1):
        before += jnp.where(owner < member, counts[slice_id, owner], 0)
    taken = counts[slice_id, member]
    for slot in range(CAP):
        tile = perm[slice_id, jnp.minimum(before + slot, TILES - 1)]
        live = slot < taken
        where = (tile // GROUP) ^ member
        here = pl.ds(pl.multiple_of((tile % GROUP) * TILE, TILE), TILE)
        target = slice(slot * TILE, (slot + 1) * TILE)
        for step in range(GROUP):

            @pl.when(live & (where == step))
            def _():
                for half, pieces in enumerate(sources):
                    out[target, half * width : (half + 1) * width] = pieces[step][here, :]

        @pl.when(jnp.logical_not(live))
        def _():
            out[target, :] = jnp.zeros((TILE, out.shape[1]), BF)


def deal_tiles(place, perm, counts, first, second, blocks):
    rows = GROUP * TILE
    specs = [pl.BlockSpec((rows, D // 2), lambda step, block=block: (block, 0)) for block in blocks for _ in first]
    return pl.pallas_call(
        deal_kernel,
        grid=(1,),
        out_shape=jax.ShapeDtypeStruct((CAP * TILE, D), BF),
        in_specs=[SM] * 3 + specs,
        out_specs=VM,
        compiler_params=params(),
        cost_estimate=HINT,
        name="deal_tiles",
    )(place, perm, counts, *first, *second)


def swap(array, axis, distance):
    count = lax.axis_size(axis)
    return lax.ppermute(array, axis, [(i, i ^ distance) for i in range(count)])


def rotary_tables(row_index, col_index):
    quarter = HEAD_DIM // 4
    inverse = 1.0 / 10000.0 ** (jnp.arange(quarter).astype(F32) * 4.0 / HEAD_DIM)
    angle = jnp.concatenate([inverse[:, None] * row_index[None], inverse[:, None] * col_index[None]], 0)
    return jnp.cos(angle), jnp.sin(angle)


def relabel(count, pair):
    where = lambda x, y, s, m: ((x * count + y) * count + s) * count + m
    span = range(count)
    route = [pair(x, y, s, m) for x in span for y in span for s in span for m in span]
    return [(where(*source), where(*target)) for source, target in route]


def gather_route(count):
    return relabel(count, lambda x, y, s, m: ((s, y, m, x), (x, y, s, m)))


def share_route(count):
    return relabel(count, lambda x, y, s, m: ((x, y, s, m), (s, y, m, x)))


def shards(
    win_query,
    win_key,
    win_value,
    win_grad_out,
    full_query,
    full_key,
    full_value,
    full_grad_out,
    proj_weight,
    positions,
    tile_perm,
    tile_counts,
):
    index = lax.axis_index("ctx")
    member, slice_id = index % GROUP, index // GROUP
    plane = slice_id // GROUP
    across = lax.axis_index("dp")
    place = jnp.stack([member, plane, slice_id]).astype(jnp.int32)
    tie = lax.optimization_barrier

    def total(arrays):
        return sum((array.astype(F32) for array in arrays[1:]), arrays[0].astype(F32))

    corner = lax.ppermute(proj_weight, ("dp", "ctx"), gather_route(GROUP))
    cos, sin = rotary_tables(positions[0, 0].astype(F32), positions[1, 0].astype(F32))
    pieces = split_heads(place, full_query[0], full_key[0], full_value[0], cos, sin)

    place, *pieces = tie((place, *pieces))
    piece1, piece2 = swap(pieces[1], "ctx", 1), swap(pieces[2], "ctx", 2)
    window_in = (win_query[0], win_key[0], win_value[0], win_grad_out[0], cos, sin)
    first = window_grads(place, *window_in, 0, (3,))

    place, first, corner, piece1, piece2, sent3 = tie((place, first, corner, piece1, piece2, pieces[3]))
    piece3 = swap(sent3, "ctx", 3)
    corners = [corner] + [swap(corner, "dp", step) for step in range(1, GROUP)]
    sibling = [swap(first[0], "ctx", 1)]
    second = window_grads(place, *window_in, 1, (1, 2))

    place, first, second, sibling, piece3, corners, grad0 = tie(
        (place, first, second, sibling, piece3, corners, full_grad_out[0])
    )
    pieces = (pieces[0], piece1, piece2, piece3)
    grad1, grad2 = swap(grad0, "ctx", 1), swap(grad0, "ctx", 2)
    low_bit, high_bit = across % 2 == 1, across // 2 == 1
    pairs = [jnp.where(low_bit, corners[i ^ 1], corners[i]) for i in range(GROUP)]
    weight0 = jnp.concatenate([jnp.where(high_bit, pairs[i ^ 2], pairs[i]) for i in range(GROUP)], 0)
    weights = [weight0] + [swap(weight0, "ctx", step * 16) for step in range(1, GROUP)]
    window = [*first, *second]
    raised_low, out, inverses = full_probs(place, pieces)

    place, raised_low, out, grad1, grad2, weights, window = tie(
        (place, raised_low, out, grad1, grad2, weights, window)
    )
    crossed = [swap(window[0], "ctx", 2)]
    sibling += [swap(array, "ctx", 1) for array in window[1:]]
    grads = (grad0, grad1, grad2, swap(grad2, "ctx", 1))
    *shares, dattn = weight_shares(place, out, grads, weights)

    place, dattn, sibling, *shares = tie((place, dattn, sibling, *shares))
    crossed.append(swap(window[1], "ctx", 2))
    swapped = [swap(shares[step], "ctx", step * 16) for step in range(1, GROUP)]
    backs = full_grads(place, pieces, dattn, out, inverses, raised_low)

    place, backs, swapped, crossed, window = tie((place, backs, swapped, crossed, window))
    part2, last = swap(backs[2], "ctx", 2), swap(window[2], "ctx", 2)
    rows = total([shares[0], *swapped]).reshape(GROUP, HEAD_DIM // GROUP, D).astype(BF)
    rows = [lax.dynamic_index_in_dim(rows, across ^ step, 0, keepdims=False) for step in range(GROUP)]
    summed = [rows[0]] + [swap(rows[step], "dp", step) for step in range(1, GROUP)]
    opposite = [swap(array, "ctx", 1) for array in crossed]

    place, summed, part2, last, opposite, sent = tie((place, summed, part2, last, opposite, (backs[1], backs[3])))
    part3, part1 = swap(sent[1], "ctx", 3), swap(sent[0], "ctx", 1)
    crossed.append(last)
    opposite.append(swap(last, "ctx", 1))
    share = total(summed).astype(BF)
    sets = list(zip(window, sibling, crossed, opposite))

    def deal(which):
        other, block = (1, 0) if which == 0 else (2, which - 1)
        return deal_tiles(place, tile_perm[0], tile_counts[0], sets[0], sets[other], (which, block))

    dealt = [deal(0), deal(1), deal(2)]
    around = [share] + [swap(share, "ctx", step * GROUP) for step in range(1, GROUP)]

    place, part1, part3, dealt, around = tie((place, part1, part3, dealt, around))
    share = lax.ppermute(total(around).astype(BF), ("dp", "ctx"), share_route(GROUP))
    full = join_heads(place, (backs[0], part1, part2, part3), cos, sin)
    return (*[array[None] for array in dealt], *[array[None] for array in full], share.astype(F32))


def solution(mesh):
    rows = P("dp", "ctx", None)
    in_specs = (rows,) * 8 + (P("ctx", None), P(None, "dp", "ctx"), P("dp", None, None), P("dp", None, None))
    out_specs = (rows,) * 6 + (P("ctx", None),)
    return jax.shard_map(shards, mesh=mesh, in_specs=in_specs, out_specs=out_specs, check_vma=False)
```

```python
import functools

import jax
import jax.numpy as jnp
from jax import lax
from jax.experimental import pallas as pl
from jax.experimental.pallas import tpu as pltpu
from jax.sharding import PartitionSpec as P

HEADS = 16
HEAD_DIM = 80
HALF = HEAD_DIM // 2
TILE = 64
TILES = 16
GROUP = 4
CAP = 8
D = HEADS * HEAD_DIM
QUARTER = D // GROUP
SCALE = HEAD_DIM**-0.5
SCALE2 = SCALE * 1.4426950408889634
BF = jnp.bfloat16
F32 = jnp.float32
VM = pl.BlockSpec(memory_space=pltpu.VMEM)
SM = pl.BlockSpec(memory_space=pltpu.SMEM)
HINT = pl.CostEstimate(flops=100_000, bytes_accessed=100_000, transcendentals=0)


def params(mib=56):
    return pltpu.CompilerParams(vmem_limit_bytes=mib << 20)


def dot(left, right, left_dim, right_dim):
    return lax.dot_general(
        left, right, (((left_dim,), (right_dim,)), ((), ())), preferred_element_type=F32
    )


def turn(rows, cos, sin):
    low, high = rows[:HALF], rows[HALF:]
    return jnp.concatenate([low * cos - high * sin, high * cos + low * sin], 0)


def turn_back(rows, cos, sin):
    low, high = rows[:HALF], rows[HALF:]
    return jnp.concatenate([low * cos + high * sin, high * cos - low * sin], 0)


def load_turned(source, target, scratch, cos, sin):
    width = source.shape[1]
    for block in range(0, width, 128):
        scratch[block : block + 128, :] = source[:, block : block + 128].astype(F32).T
    for head in range(0, width, HEAD_DIM):
        rows = scratch[head : head + HEAD_DIM, :]
        if cos is not None:
            rows = turn(rows, cos, sin)
        target[head : head + HEAD_DIM, :] = rows.astype(BF)


def store_natural(scratch, target):
    for block in range(0, scratch.shape[0], 128):
        target[:, block : block + 128] = scratch[block : block + 128, :].T.astype(BF)


def split_kernel(place, query, key, value, cos_ref, sin_ref, out0, out1, out2, out3, scratch, qt, kt, vt):
    cos, sin = cos_ref[...], sin_ref[...]
    load_turned(query, qt, scratch, cos, sin)
    load_turned(key, kt, scratch, cos, sin)
    load_turned(value, vt, scratch, None, None)
    member = place[0]
    for step, out in enumerate((out0, out1, out2, out3)):
        for part, source in enumerate((qt, kt, vt)):
            for block in range(GROUP):
                start = pl.multiple_of((member ^ step) * HEAD_DIM + block * QUARTER, HEAD_DIM)
                target = part * QUARTER + block * HEAD_DIM
                out[target : target + HEAD_DIM, :] = source[pl.ds(start, HEAD_DIM), :]


def split_heads(place, query, key, value, cos, sin):
    rows = query.shape[0]
    return pl.pallas_call(
        split_kernel,
        out_shape=[jax.ShapeDtypeStruct((3 * QUARTER, rows), BF)] * GROUP,
        in_specs=[SM] + [VM] * 5,
        out_specs=[VM] * GROUP,
        scratch_shapes=[pltpu.VMEM((D, rows), F32)] + [pltpu.VMEM((D, rows), BF)] * 3,
        compiler_params=params(),
        cost_estimate=HINT,
        name="split_heads",
    )(place, query, key, value, cos, sin)


def window_kernel(place, query, key, value, grad, cos_ref, sin_ref, *refs):
    del place
    outs, (scratch, qt, kt, vt, gt, dqt, dkt, dvt) = refs[:-8], refs[-8:]
    cos, sin = cos_ref[...], sin_ref[...]
    load_turned(query, qt, scratch, cos, sin)
    load_turned(key, kt, scratch, cos, sin)
    load_turned(value, vt, scratch, None, None)
    load_turned(grad, gt, scratch, None, None)
    rows, width = query.shape
    same = (
        lax.broadcasted_iota(jnp.int32, (rows, rows), 0) // TILE
        == lax.broadcasted_iota(jnp.int32, (rows, rows), 1) // TILE
    )

    def head_step(head, carry):
        here = pl.ds(pl.multiple_of(head * HEAD_DIM, HEAD_DIM), HEAD_DIM)
        q, k, v, g = qt[here, :], kt[here, :], vt[here, :], gt[here, :]
        logits = jnp.where(same, dot(k, q, 0, 0), -1e30)
        raised = jnp.exp2((logits - jnp.max(logits, 0, keepdims=True)) * SCALE2)
        inverse = 1.0 / jnp.sum(raised, 0, keepdims=True)
        low = raised.astype(BF)
        g = (g.astype(F32) * inverse).astype(BF)
        center = jnp.sum(g.astype(F32) * (dot(v, low, 1, 0) * inverse), 0, keepdims=True)
        dscores = (raised * (dot(v, g, 0, 0) - center)).astype(BF)
        dqt[here, :] = turn_back(dot(k, dscores, 1, 0) * SCALE, cos, sin)
        dkt[here, :] = turn_back(dot(q, dscores, 1, 1) * SCALE, cos, sin)
        dvt[here, :] = dot(g, low, 1, 1)
        return carry

    lax.fori_loop(0, width // HEAD_DIM, head_step, 0, unroll=2)
    places = [out.at[at : at + rows] for out in outs for at in range(0, out.shape[0], rows)]
    for source, target in zip((dqt, dkt, dvt), places):
        store_natural(source, target)


def window_grads(place, query, key, value, grad, cos, sin, half, packs):
    rows, width = query.shape[0], D // 2
    block = pl.BlockSpec((rows, width), lambda step: (0, half))
    return pl.pallas_call(
        window_kernel,
        grid=(1,),
        out_shape=[jax.ShapeDtypeStruct((pack * rows, width), BF) for pack in packs],
        in_specs=[SM] + [block] * 4 + [VM] * 2,
        out_specs=[VM] * len(packs),
        scratch_shapes=[pltpu.VMEM((width, rows), F32)] + [pltpu.VMEM((width, rows), BF)] * 4 + [pltpu.VMEM((width, rows), F32)] * 3,
        compiler_params=params(),
        cost_estimate=HINT,
        name="window_grads",
    )(place, query, key, value, grad, cos, sin)


def heads_of(pieces, first, part, width):
    rows = pl.ds(pl.multiple_of(first + part * width, 16), HEAD_DIM)
    return jnp.concatenate([piece[rows, :] for piece in pieces], 1)


def probs_kernel(place, piece0, piece1, piece2, piece3, raised_low, out, inverses):
    del place
    pieces = (piece0, piece1, piece2, piece3)
    rows = piece0.shape[1]
    first = pl.multiple_of(pl.program_id(0) * HEAD_DIM, HEAD_DIM)
    here = pl.ds(first, HEAD_DIM)
    k_rows, v = heads_of(pieces, first, 1, QUARTER).T, heads_of(pieces, first, 2, QUARTER)
    for step in range(GROUP):
        block = slice(step * rows, (step + 1) * rows)
        logits = dot(k_rows, pieces[step][here, :], 1, 0)
        raised = jnp.exp2((logits - jnp.max(logits, 0, keepdims=True)) * SCALE2)
        inverse = 1.0 / jnp.sum(raised, 0, keepdims=True)
        low = raised.astype(BF)
        raised_low[0, :, block] = low
        inverses[pl.program_id(0), :, block] = inverse
        out[here, block] = dot(v, low, 1, 0) * inverse


def full_probs(place, pieces):
    length = GROUP * pieces[0].shape[1]
    heads = HEADS // GROUP
    return pl.pallas_call(
        probs_kernel,
        grid=(heads,),
        out_shape=[
            jax.ShapeDtypeStruct((heads, length, length), BF),
            jax.ShapeDtypeStruct((QUARTER, length), F32),
            jax.ShapeDtypeStruct((heads, 1, length), F32),
        ],
        in_specs=[SM] + [VM] * 4,
        out_specs=[pl.BlockSpec((1, length, length), lambda head: (head, 0, 0)), VM, VM],
        compiler_params=params(),
        cost_estimate=HINT,
        name="full_probs",
    )(place, *pieces)


def share_kernel(*refs):
    place, out, grads, weights, shares, dattn = refs[0], refs[1], refs[2:6], refs[6:10], refs[10:14], refs[14]
    product, weight = refs[15:]
    rows = grads[0].shape[0]
    starts = [pl.multiple_of((place[1] ^ step) * HEAD_DIM, HEAD_DIM) for step in range(GROUP)]
    for step in range(GROUP):
        weight[pl.ds(starts[step], HEAD_DIM), :] = weights[step][...]
    for step in range(GROUP):
        block = slice(step * rows, (step + 1) * rows)
        dattn[:, block] = dot(weight[...], grads[step][...], 1, 1).astype(BF)
        share = dot(out[:, block].astype(BF), grads[step][...], 1, 0)
        product[...] = share if step == 0 else product[...] + share
    for step in range(GROUP):
        shares[step][...] = product[pl.ds(starts[step], HEAD_DIM), :].astype(BF)


def weight_shares(place, out, grads, weights):
    return pl.pallas_call(
        share_kernel,
        out_shape=[jax.ShapeDtypeStruct((HEAD_DIM, D), BF)] * GROUP + [jax.ShapeDtypeStruct(out.shape, BF)],
        in_specs=[SM] + [VM] * 9,
        out_specs=[VM] * 5,
        scratch_shapes=[pltpu.VMEM((QUARTER, D), F32), pltpu.VMEM((QUARTER, D), BF)],
        compiler_params=params(),
        cost_estimate=HINT,
        name="weight_shares",
    )(place, out, *grads, *weights)


def grads_kernel(*refs):
    pieces, dattn, out, inverses, raised_low, backs = refs[1:5], refs[5], refs[6], refs[7], refs[8], refs[9:]
    rows = pieces[0].shape[1]
    first = pl.multiple_of(pl.program_id(0) * HEAD_DIM, HEAD_DIM)
    here = pl.ds(first, HEAD_DIM)
    k, v_rows = heads_of(pieces, first, 1, QUARTER), heads_of(pieces, first, 2, QUARTER).T
    dk = jnp.zeros((HEAD_DIM, GROUP * rows), F32)
    dv = jnp.zeros((HEAD_DIM, GROUP * rows), F32)
    for step in range(GROUP):
        block = slice(step * rows, (step + 1) * rows)
        q, low = pieces[step][here, :], raised_low[0, :, block]
        g = (dattn[here, block].astype(F32) * inverses[pl.program_id(0), :, block]).astype(BF)
        center = jnp.sum(g.astype(F32) * out[here, block], 0, keepdims=True)
        dscores = (low.astype(F32) * (dot(v_rows, g, 1, 0) - center)).astype(BF)
        backs[step][here, :] = (dot(k, dscores, 1, 0) * SCALE).astype(BF)
        dk += dot(q, dscores, 1, 1)
        dv += dot(g, low, 1, 1)
    for step in range(GROUP):
        block = slice(step * rows, (step + 1) * rows)
        backs[step][pl.ds(pl.multiple_of(first + QUARTER, 16), HEAD_DIM), :] = (dk[:, block] * SCALE).astype(BF)
        backs[step][pl.ds(pl.multiple_of(first + 2 * QUARTER, 16), HEAD_DIM), :] = dv[:, block].astype(BF)


def full_grads(place, pieces, dattn, out, inverses, raised_low):
    rows = pieces[0].shape[1]
    length = GROUP * rows
    return pl.pallas_call(
        grads_kernel,
        grid=(HEADS // GROUP,),
        out_shape=[jax.ShapeDtypeStruct((3 * QUARTER, rows), BF)] * GROUP,
        in_specs=[SM] + [VM] * 7 + [pl.BlockSpec((1, length, length), lambda head: (head, 0, 0))],
        out_specs=[VM] * GROUP,
        compiler_params=params(),
        cost_estimate=HINT,
        name="full_grads",
    )(place, *pieces, dattn, out, inverses, raised_low)


def join_kernel(place, part0, part1, part2, part3, cos_ref, sin_ref, dquery, dkey, dvalue, scratch):
    cos, sin = cos_ref[...], sin_ref[...]
    member = place[0]
    for which, target in enumerate((dquery, dkey, dvalue)):
        for step, part in enumerate((part0, part1, part2, part3)):
            for block in range(GROUP):
                source = which * QUARTER + block * HEAD_DIM
                rows = part[source : source + HEAD_DIM, :].astype(F32)
                if which < 2:
                    rows = turn_back(rows, cos, sin)
                start = pl.multiple_of((member ^ step) * HEAD_DIM + block * QUARTER, HEAD_DIM)
                scratch[pl.ds(start, HEAD_DIM), :] = rows
        store_natural(scratch, target)


def join_heads(place, parts, cos, sin):
    rows = parts[0].shape[1]
    return pl.pallas_call(
        join_kernel,
        out_shape=[jax.ShapeDtypeStruct((rows, D), BF)] * 3,
        in_specs=[SM] + [VM] * 6,
        out_specs=[VM] * 3,
        scratch_shapes=[pltpu.VMEM((D, rows), F32)],
        compiler_params=params(),
        cost_estimate=HINT,
        name="join_heads",
    )(place, *parts, cos, sin)


def deal_kernel(place, perm, counts, *refs):
    sources, out = (refs[:GROUP], refs[GROUP : 2 * GROUP]), refs[2 * GROUP]
    member, slice_id = place[0], place[2]
    width = sources[0][0].shape[1]
    before = jnp.int32(0)
    for owner in range(GROUP - 1):
        before += jnp.where(owner < member, counts[slice_id, owner], 0)
    taken = counts[slice_id, member]
    for slot in range(CAP):
        tile = perm[slice_id, jnp.minimum(before + slot, TILES - 1)]
        live = slot < taken
        where = (tile // GROUP) ^ member
        here = pl.ds(pl.multiple_of((tile % GROUP) * TILE, TILE), TILE)
        target = slice(slot * TILE, (slot + 1) * TILE)
        for step in range(GROUP):

            @pl.when(live & (where == step))
            def _():
                for half, pieces in enumerate(sources):
                    out[target, half * width : (half + 1) * width] = pieces[step][here, :]

        @pl.when(jnp.logical_not(live))
        def _():
            out[target, :] = jnp.zeros((TILE, out.shape[1]), BF)


def deal_tiles(place, perm, counts, first, second, blocks):
    rows = GROUP * TILE
    specs = [pl.BlockSpec((rows, D // 2), lambda step, block=block: (block, 0)) for block in blocks for _ in first]
    return pl.pallas_call(
        deal_kernel,
        grid=(1,),
        out_shape=jax.ShapeDtypeStruct((CAP * TILE, D), BF),
        in_specs=[SM] * 3 + specs,
        out_specs=VM,
        compiler_params=params(),
        cost_estimate=HINT,
        name="deal_tiles",
    )(place, perm, counts, *first, *second)


def swap(array, axis, distance):
    count = lax.axis_size(axis)
    return lax.ppermute(array, axis, [(i, i ^ distance) for i in range(count)])


def rotary_tables(row_index, col_index):
    quarter = HEAD_DIM // 4
    inverse = 1.0 / 10000.0 ** (jnp.arange(quarter).astype(F32) * 4.0 / HEAD_DIM)
    angle = jnp.concatenate([inverse[:, None] * row_index[None], inverse[:, None] * col_index[None]], 0)
    return jnp.cos(angle), jnp.sin(angle)


def relabel(count, pair):
    where = lambda x, y, s, m: ((x * count + y) * count + s) * count + m
    span = range(count)
    route = [pair(x, y, s, m) for x in span for y in span for s in span for m in span]
    return [(where(*source), where(*target)) for source, target in route]


def gather_route(count):
    return relabel(count, lambda x, y, s, m: ((s, y, m, x), (x, y, s, m)))


def share_route(count):
    return relabel(count, lambda x, y, s, m: ((x, y, s, m), (s, y, m, x)))


def shards(
    win_query,
    win_key,
    win_value,
    win_grad_out,
    full_query,
    full_key,
    full_value,
    full_grad_out,
    proj_weight,
    positions,
    tile_perm,
    tile_counts,
):
    index = lax.axis_index("ctx")
    member, slice_id = index % GROUP, index // GROUP
    plane = slice_id // GROUP
    across = lax.axis_index("dp")
    place = jnp.stack([member, plane, slice_id]).astype(jnp.int32)
    tie = lax.optimization_barrier

    def total(arrays):
        return sum((array.astype(F32) for array in arrays[1:]), arrays[0].astype(F32))

    corner = lax.ppermute(proj_weight, ("dp", "ctx"), gather_route(GROUP))
    cos, sin = rotary_tables(positions[0, 0].astype(F32), positions[1, 0].astype(F32))
    pieces = split_heads(place, full_query[0], full_key[0], full_value[0], cos, sin)

    place, *pieces = tie((place, *pieces))
    piece1, piece2 = swap(pieces[1], "ctx", 1), swap(pieces[2], "ctx", 2)
    window_in = (win_query[0], win_key[0], win_value[0], win_grad_out[0], cos, sin)
    first = window_grads(place, *window_in, 0, (3,))

    place, first, corner, piece1, piece2, sent3 = tie((place, first, corner, piece1, piece2, pieces[3]))
    piece3 = swap(sent3, "ctx", 3)
    corners = [corner] + [swap(corner, "dp", step) for step in range(1, GROUP)]
    sibling = [swap(first[0], "ctx", 1)]
    second = window_grads(place, *window_in, 1, (1, 2))

    place, first, second, sibling, piece3, corners, grad0 = tie(
        (place, first, second, sibling, piece3, corners, full_grad_out[0])
    )
    pieces = (pieces[0], piece1, piece2, piece3)
    grad1, grad2 = swap(grad0, "ctx", 1), swap(grad0, "ctx", 2)
    low_bit, high_bit = across % 2 == 1, across // 2 == 1
    pairs = [jnp.where(low_bit, corners[i ^ 1], corners[i]) for i in range(GROUP)]
    weight0 = jnp.concatenate([jnp.where(high_bit, pairs[i ^ 2], pairs[i]) for i in range(GROUP)], 0)
    weights = [weight0] + [swap(weight0, "ctx", step * 16) for step in range(1, GROUP)]
    window = [*first, *second]
    raised_low, out, inverses = full_probs(place, pieces)

    place, raised_low, out, grad1, grad2, weights, window = tie(
        (place, raised_low, out, grad1, grad2, weights, window)
    )
    crossed = [swap(window[0], "ctx", 2)]
    sibling += [swap(array, "ctx", 1) for array in window[1:]]
    grads = (grad0, grad1, grad2, swap(grad2, "ctx", 1))
    *shares, dattn = weight_shares(place, out, grads, weights)

    place, dattn, sibling, *shares = tie((place, dattn, sibling, *shares))
    crossed.append(swap(window[1], "ctx", 2))
    swapped = [swap(shares[step], "ctx", step * 16) for step in range(1, GROUP)]
    backs = full_grads(place, pieces, dattn, out, inverses, raised_low)

    place, backs, swapped, crossed, window = tie((place, backs, swapped, crossed, window))
    part2, last = swap(backs[2], "ctx", 2), swap(window[2], "ctx", 2)
    rows = total([shares[0], *swapped]).reshape(GROUP, HEAD_DIM // GROUP, D).astype(BF)
    rows = [lax.dynamic_index_in_dim(rows, across ^ step, 0, keepdims=False) for step in range(GROUP)]
    summed = [rows[0]] + [swap(rows[step], "dp", step) for step in range(1, GROUP)]
    opposite = [swap(array, "ctx", 1) for array in crossed]
    part1 = swap(backs[1], "ctx", 1)

    def deal(which):
        sets = list(zip(window, sibling, crossed, opposite))
        other, block = (1, 0) if which == 0 else (2, which - 1)
        return deal_tiles(place, tile_perm[0], tile_counts[0], sets[0], sets[other], (which, block))

    dealt = [deal(0)]

    place, summed, part1, part2, last, opposite, dealt, sent = tie(
        (place, summed, part1, part2, last, opposite, dealt, backs[3])
    )
    part3 = swap(sent, "ctx", 3)
    crossed.append(last)
    opposite.append(swap(last, "ctx", 1))
    share = total(summed).astype(BF)
    around = [share] + [swap(share, "ctx", step * GROUP) for step in range(1, GROUP)]

    place, part3, opposite, around = tie((place, part3, opposite, around))
    share = lax.ppermute(total(around).astype(BF), ("dp", "ctx"), share_route(GROUP))
    full = join_heads(place, (backs[0], part1, part2, part3), cos, sin)
    dealt += [deal(1), deal(2)]
    return (*[array[None] for array in dealt], *[array[None] for array in full], share.astype(F32))


def solution(mesh):
    rows = P("dp", "ctx", None)
    in_specs = (rows,) * 8 + (P("ctx", None), P(None, "dp", "ctx"), P("dp", None, None), P("dp", None, None))
    out_specs = (rows,) * 6 + (P("ctx", None),)
    return jax.shard_map(shards, mesh=mesh, in_specs=in_specs, out_specs=out_specs, check_vma=False)
```
